32 devices in a mesh: sec: 2 (over core), gx: 4 (over z), gy: 4 (over y, x).
Axes of the slice: x: 2, y: 2, z: 4, core: 2. Of those that a mesh axis runs over, the one named last changes fastest.
Arguments:
- terminal: float32 [4, 16, 64, 1024], P('sec', None, 'gx', 'gy'), may hold values from -6 to 6
- forward_temp: bfloat16 [2, 4, 16, 64, 1024], P(None, 'sec', None, 'gx', 'gy'), may hold values from -6 to 6
- conductivity: float32 [16, 64, 1024], P(None, 'gx', 'gy'), may hold values from 0.02 to 0.15
- velocity: float32 [2, 16, 64, 1024], P(None, None, 'gx', 'gy'), may hold values from -0.3 to 0.3
- fixed_mask: int32 [16, 64, 1024], P(None, 'gx', 'gy'), may hold values 0 or 1
- wells: int32 [4, 8, 3], P('sec'), may hold values from 0 to 1023, as said below
- misfit: float32 [2, 4, 8], P(None, 'sec'), may hold values from -12 to 12
- head_gradient: bfloat16 [2, 16, 64, 1024], P('sec', None, 'gx', 'gy'), may hold values from -6 to 6
- blocks: bfloat16 [8, 7, 128, 128], P('gy'), may hold values from -0.1875 to 0.1875
- block_cols: int32 [8, 7], P('gy'), may hold values from 0 to 7, as said below
Outputs:
- head_adjoint: float32 [2, 16, 64, 1024], P('sec', None, 'gx', 'gy')
- sensitivity: float32 [16, 64, 1024], P(None, 'gx', 'gy')
The draws below stay inside these ranges and needn't reach their ends.
Inputs may be any that keep to these rules, and one draw needn't show every extreme that they name: `wells`: each row is one cell (z, x, y) with z < 16, x < 64, y < 1024; the first test observes the cells (0, 0, 0) and (15, 63, 1023). `block_cols`: row r lists 7 different block columns, the first of which is r.
All inputs are finite; a program needn't handle non-finite values. No bound on the sum of `fixed_mask` on one device may be relied on, other than what follows from the above.
Results may differ from the reference program's by a relative error of at most 0.0029.
Values may be sent and summed in bfloat16 or wider, within the bound.
A program may use at most 64 MiB of HBM per device.

```python
import math
import jax
import jax.numpy as jnp
from jax import lax

NZ = 16
BLOCK = 128
NNZB = 7
TESTS = 4
STEPS = 2
WELLS = 8
NX = 64
NY = 1024
NBY = 8


def draw_wells(key, part):
    key_z, key_x, key_y = jax.random.split(jax.random.fold_in(key, 11), 3)
    coord_z = jax.random.randint(key_z, (TESTS, WELLS, 1), 0, NZ, dtype=jnp.int32)
    coord_x = jax.random.randint(key_x, (TESTS, WELLS, 1), 0, NX, dtype=jnp.int32)
    coord_y = jax.random.randint(key_y, (TESTS, WELLS, 1), 0, NY, dtype=jnp.int32)
    cells = jnp.concatenate([coord_z, coord_x, coord_y], axis=2).astype(jnp.int32)
    cells = cells.at[0, 0, :].set(jnp.zeros((3,), jnp.int32))
    corner = jnp.array([NZ - 1, NX - 1, NY - 1], dtype=jnp.int32)
    cells = cells.at[0, 1, :].set(corner)
    return cells.astype(jnp.int32)


def draw_block_cols(key, part):
    scores = jax.random.randint(jax.random.fold_in(key, 23), (NBY, NBY), 0, 2 ** 20, dtype=jnp.int32)
    scores = scores * NBY + jnp.arange(NBY, dtype=jnp.int32)[None, :]
    scores = jnp.where(jnp.eye(NBY, dtype=bool), -1, scores)
    order = jnp.argsort(scores, axis=1)
    return order[:, :NNZB].astype(jnp.int32)


def plant(drawn, rng, smallest, top_value):
    shape = drawn.shape
    place = [jax.random.randint(jax.random.fold_in(rng, axis), (), 0, shape[axis]) for axis in range(len(shape))]
    drawn = drawn.at[tuple(place)].set(smallest)
    longest = shape.index(max(shape))
    place[longest] = (place[longest] + 1) % shape[longest]
    return drawn.at[tuple(place)].set(top_value)


def shard_levels(rng, extent, cuts, smallest, largest):
    level, own = 1.0, jax.random.fold_in(rng, 6)
    for axis_at, blocks in cuts:
        steps = jnp.exp(jax.random.uniform(jax.random.fold_in(own, axis_at), (blocks,), jnp.float32, smallest / len(cuts), largest / len(cuts)))
        level = level * jnp.repeat(steps, extent[axis_at] // blocks).reshape([-1 if axis == axis_at else 1 for axis in range(len(extent))])
    return level


def normal_values(key, extent, width, bound, cuts=(), held_as=jnp.bfloat16):
    entries = jax.random.normal(key, extent, jnp.float32) * width
    if len(cuts) > 0:
        entries = shard_levels(key, extent, cuts, -0.22, 0.18) * entries
    return jnp.clip(entries, min=-bound, max=bound).astype(held_as)


def setup_inputs(seed: int = 0) -> dict:
    splits = jax.random.split(jax.random.key(seed), 11)
    return {
        "terminal": normal_values(splits[0], (TESTS, NZ, NX, NY), 1.0, 6.0, ((0, 2), (2, 4), (3, 4)), jnp.float32),
        "forward_temp": normal_values(splits[1], (STEPS, TESTS, NZ, NX, NY), 1.0, 6.0, ((1, 2), (3, 4), (4, 4))),
        "conductivity": jnp.clip(jnp.exp(math.log(0.15) - 2.014903 * jax.random.uniform(splits[2], (NZ, NX, NY), jnp.float32) ** shard_levels(splits[2], (NZ, NX, NY), ((1, 4), (2, 4)), -0.2, 0.2)), 0.02, 0.15),
        "velocity": jnp.clip(jax.random.uniform(splits[3], (2, NZ, NX, NY), jnp.float32, -0.3, 0.3) * shard_levels(splits[3], (2, NZ, NX, NY), ((2, 4), (3, 4)), -0.4, 0.0), -0.3, 0.3),
        "fixed_mask": plant((jax.random.randint(splits[4], (NZ, NX, NY), 0, 8) < 1).astype(jnp.int32), jax.random.fold_in(splits[4], 1), 0, 1),
        "wells": draw_wells(jax.random.fold_in(splits[10], 71), 0),
        "misfit": normal_values(splits[6], (STEPS, TESTS, WELLS), 3.0, 12.0, ((1, 2),), jnp.float32),
        "head_gradient": normal_values(splits[7], (2, NZ, NX, NY), 1.0, 6.0, ((0, 2), (2, 4), (3, 4))),
        "blocks": normal_values(splits[8], (NBY, NNZB, BLOCK, BLOCK), (NNZB * BLOCK) ** -0.5, 0.1875, ((0, 4),)),
        "block_cols": draw_block_cols(jax.random.fold_in(splits[10], 71), 0),
    }


def shifted(padded):
    lead = [(0, 0)] * (padded.ndim - 3)
    deeper = jnp.pad(padded, lead + [(1, 1), (0, 0), (0, 0)])
    centre = deeper[..., 1:-1, 1:-1, 1:-1]
    beside_all = [deeper[..., 2:, 1:-1, 1:-1], deeper[..., :-2, 1:-1, 1:-1],
              deeper[..., 1:-1, 2:, 1:-1], deeper[..., 1:-1, :-2, 1:-1],
              deeper[..., 1:-1, 1:-1, 2:], deeper[..., 1:-1, 1:-1, :-2]]
    return centre, beside_all


def face_weights(kappa_pad):
    centre, beside_all = shifted(kappa_pad)
    return [2.0 * centre * other / jnp.where(centre + other > 0.0, centre + other, 1.0) for other in beside_all]


def advance(adjoint_pad, weights, keep, speed_x, speed_y, source):
    centre, beside_all = shifted(adjoint_pad)
    diffusion = weights[0] * (beside_all[0] - centre)
    for face in range(1, 6):
        diffusion = diffusion + weights[face] * (beside_all[face] - centre)
    slope_x = 0.5 * (beside_all[2] - beside_all[3])
    slope_y = 0.5 * (beside_all[4] - beside_all[5])
    updated = keep * (centre + diffusion + speed_x * slope_x + speed_y * slope_y + source)
    return updated, diffusion, slope_x, slope_y


def reference(terminal, forward_temp, conductivity, velocity, fixed_mask, wells, misfit, head_gradient, blocks, block_cols):
    keep = 1.0 - fixed_mask.astype(jnp.float32)
    weights = face_weights(jnp.pad(conductivity, ((0, 0), (1, 1), (1, 1))))
    heat_sens = jnp.zeros((NZ, NX, NY), jnp.float32)
    flow_x = jnp.zeros((NZ, NX, NY), jnp.float32)
    flow_y = jnp.zeros((NZ, NX, NY), jnp.float32)
    for test in range(TESTS):
        adjoint = terminal[test]
        for level in reversed(range(STEPS)):
            source = jnp.zeros((NZ, NX, NY), jnp.float32).at[wells[test, :, 0], wells[test, :, 1], wells[test, :, 2]].add(misfit[level, test])
            padded = jnp.pad(adjoint, ((0, 0), (1, 1), (1, 1)))
            adjoint, diffusion, slope_x, slope_y = advance(padded, weights, keep, velocity[0], velocity[1], source)
            temper = forward_temp[level, test].astype(jnp.float32)
            heat_sens = heat_sens + temper * diffusion
            flow_x = flow_x + temper * slope_x
            flow_y = flow_y + temper * slope_y
    rounded = jnp.stack([flow_x, flow_y]).astype(jnp.bfloat16)
    heads = []
    for comp in range(2):
        flat = rounded[comp].reshape(NZ * NX, NBY, BLOCK)

        def one_row(index):
            chosen = jnp.take(flat, block_cols[index], axis=1).astype(jnp.float32)
            return jnp.einsum('rkj,kij->ri', chosen, blocks[index].astype(jnp.float32), precision=lax.Precision.HIGHEST)

        per_row = lax.map(one_row, jnp.arange(NBY, dtype=jnp.int32))
        heads.append(jnp.transpose(per_row, (1, 0, 2)).reshape(NZ, NX, NY))
    head_adjoint = jnp.stack(heads)
    sensitivity = heat_sens + head_adjoint[0] * head_gradient[0].astype(jnp.float32) + head_adjoint[1] * head_gradient[1].astype(jnp.float32)
    return head_adjoint, sensitivity
```

```python
import functools

import jax
import jax.numpy as jnp
from jax import lax
from jax.experimental import pallas as pl
from jax.experimental.pallas import tpu as pltpu
from jax.sharding import PartitionSpec as P

MESH = pl.DeviceIdType.MESH
LANES = 128
CHUNKS = 4
NT = (((1,), (1,)), ((), ()))


def kernel(
    n_gx, n_gy, wells, misfit, cols, term, fwd, kappa, vel, mask, grad, blocks,
    head, sens, wgt, adj, heat, flow, flow_in, part, part_in,
    sx1, sy1, hx1, hy1, sx2, sy2, hx2, hy2,
    h_send, h_recv, f_send, f_recv, g_send, g_recv, p_send, p_recv, *gath,
):
    tests, layers, rows, width = term.shape
    row_blocks, per_row, size, _ = blocks.shape
    per = layers // CHUNKS
    s, gx, gy = lax.axis_index("sec"), lax.axis_index("gx"), lax.axis_index("gy")
    other = 1 - s
    exists = (gx > 0, gx < n_gx - 1, gy > 0, gy < n_gy - 1)
    target = (
        {"gx": jnp.maximum(gx - 1, 0)}, {"gx": jnp.minimum(gx + 1, n_gx - 1)},
        {"gy": jnp.maximum(gy - 1, 0)}, {"gy": jnp.minimum(gy + 1, n_gy - 1)},
    )

    row_id = lax.broadcasted_iota(jnp.int32, (rows, width), 0)
    col_id = lax.broadcasted_iota(jnp.int32, (rows, width), 1)
    lane = lax.broadcasted_iota(jnp.int32, (rows, LANES), 1)

    barrier = pltpu.get_barrier_semaphore()
    for side in (0, 1):
        @pl.when(exists[side])
        def _(side=side):
            pl.semaphore_signal(barrier, 1, device_id=target[side], device_id_type=MESH)
    for off in range(1, n_gy):
        pl.semaphore_signal(barrier, 1, device_id={"gy": lax.rem(gy + off, n_gy)}, device_id_type=MESH)
    pl.semaphore_signal(barrier, 1, device_id={"sec": other}, device_id_type=MESH)

    def halo(round_, side, sx, sy, hx, hy):
        opposite = side ^ 1
        src = sx.at[side] if side < 2 else sy.at[side - 2]
        dst = hx.at[opposite] if side < 2 else hy.at[opposite - 2]
        return pltpu.make_async_remote_copy(
            src_ref=src, dst_ref=dst,
            send_sem=h_send.at[round_, side], recv_sem=h_recv.at[round_, opposite],
            device_id=target[side], device_id_type=MESH,
        )

    def halo_recv(round_, side, sx, sy, hx, hy):
        src = sx.at[side] if side < 2 else sy.at[side - 2]
        dst = hx.at[side] if side < 2 else hy.at[side - 2]
        return pltpu.make_async_remote_copy(
            src_ref=src, dst_ref=dst,
            send_sem=h_send.at[round_, side], recv_sem=h_recv.at[round_, side],
            device_id=target[side], device_id_type=MESH,
        )

    def start_halo(round_, bufs):
        for side in range(4):
            @pl.when(exists[side])
            def _(side=side):
                halo(round_, side, *bufs).start()

    def wait_halo(round_, bufs):
        for side in range(4):
            @pl.when(exists[side])
            def _(side=side):
                halo_recv(round_, side, *bufs).wait()

            @pl.when(jnp.logical_not(exists[side]))
            def _(side=side):
                into = bufs[2].at[side] if side < 2 else bufs[3].at[side - 2]
                into[...] = jnp.zeros(into.shape, jnp.float32)

    zero = jnp.zeros((rows, LANES), jnp.float32)

    def pack1(z, carry):
        low, high = carry
        planes = [term[t, z] for t in range(tests)] + [kappa[z]]
        for slot, plane in enumerate(planes):
            here = lane == slot * layers + z
            low = jnp.where(here, plane[:, 0:1], low)
            high = jnp.where(here, plane[:, width - 1:width], high)
            sx1[0, slot, pl.ds(z, 1), :] = plane[0:1, :]
            sx1[1, slot, pl.ds(z, 1), :] = plane[rows - 1:rows, :]
        return low, high

    low, high = lax.fori_loop(0, layers, pack1, (zero, zero))
    sy1[0] = low
    sy1[1] = high
    expected = n_gy + (gx > 0).astype(jnp.int32) + (gx < n_gx - 1).astype(jnp.int32)
    pl.semaphore_wait(barrier, expected)
    bufs1 = (sx1, sy1, hx1, hy1)
    bufs2 = (sx2, sy2, hx2, hy2)
    start_halo(0, bufs1)

    cell = row_id * width + col_id
    plane_cells = rows * width
    marks = []
    for t in range(tests):
        for w in range(wells.shape[1]):
            lx = wells[t, w, 1] - gx * rows
            ly = wells[t, w, 2] - gy * width
            inside = (lx >= 0) & (lx < rows) & (ly >= 0) & (ly < width)
            place = wells[t, w, 0] * plane_cells + lx * width + ly
            marks.append(jnp.where(inside, place, -1))

    def sources(z, _):
        now = cell + z * plane_cells
        for t in range(tests):
            total = jnp.zeros((rows, width), jnp.float32)
            for w in range(wells.shape[1]):
                total = total + jnp.where(now == marks[t * wells.shape[1] + w], misfit[1, t, w], 0.0)
            adj[t, z] = total
        return 0

    lax.fori_loop(0, layers, sources, 0)
    wait_halo(0, bufs1)

    def picked_lane(ref, side, index):
        return jnp.sum(jnp.where(lane == index, ref[side], 0.0), axis=1, keepdims=True)

    def beside(plane, hx, hy, slot, z):
        xp = jnp.where(row_id == rows - 1, hx[1, slot, pl.ds(z, 1), :], pltpu.roll(plane, rows - 1, 0))
        xm = jnp.where(row_id == 0, hx[0, slot, pl.ds(z, 1), :], pltpu.roll(plane, 1, 0))
        index = slot * layers + z
        yp = jnp.where(col_id == width - 1, picked_lane(hy, 1, index), pltpu.roll(plane, width - 1, 1))
        ym = jnp.where(col_id == 0, picked_lane(hy, 0, index), pltpu.roll(plane, 1, 1))
        return xp, xm, yp, ym

    def harmonic(a, b):
        return 2.0 * a * b / (a + b)

    def first(z, carry):
        low, high = carry
        zp, zm = jnp.minimum(z + 1, layers - 1), jnp.maximum(z - 1, 0)
        k = kappa[z]
        weights = [harmonic(k, kappa[zp]), harmonic(k, kappa[zm])]
        weights += [harmonic(k, near) for near in beside(k, hx1, hy1, tests, z)]
        for face in range(6):
            wgt[face, z] = weights[face]
        keep = 1.0 - mask[z].astype(jnp.float32)
        hs = jnp.zeros((rows, width), jnp.float32)
        fx, fy = hs, hs
        for t in range(tests):
            c = term[t, z]
            near = (term[t, zp], term[t, zm]) + beside(c, hx1, hy1, t, z)
            diff = weights[0] * (near[0] - c)
            for face in range(1, 6):
                diff = diff + weights[face] * (near[face] - c)
            slope_x = 0.5 * (near[2] - near[3])
            slope_y = 0.5 * (near[4] - near[5])
            new = keep * (c + diff + vel[0, z] * slope_x + vel[1, z] * slope_y + adj[t, z])
            adj[t, z] = new
            here = lane == t * layers + z
            low = jnp.where(here, new[:, 0:1], low)
            high = jnp.where(here, new[:, width - 1:width], high)
            sx2[0, t, pl.ds(z, 1), :] = new[0:1, :]
            sx2[1, t, pl.ds(z, 1), :] = new[rows - 1:rows, :]
            temper = fwd[1, t, z].astype(jnp.float32)
            hs = hs + temper * diff
            fx = fx + temper * slope_x
            fy = fy + temper * slope_y
        heat[z] = hs
        flow[0, z] = fx
        flow[1, z] = fy
        return low, high

    low, high = lax.fori_loop(0, layers, first, (zero, zero))
    sy2[0] = low
    sy2[1] = high
    start_halo(1, bufs2)
    wait_halo(1, bufs2)

    def second(z, _):
        zp, zm = jnp.minimum(z + 1, layers - 1), jnp.maximum(z - 1, 0)
        hs, fx, fy = heat[z], flow[0, z], flow[1, z]
        for t in range(tests):
            c = adj[t, z]
            near = (adj[t, zp], adj[t, zm]) + beside(c, hx2, hy2, t, z)
            diff = wgt[0, z] * (near[0] - c)
            for face in range(1, 6):
                diff = diff + wgt[face, z] * (near[face] - c)
            temper = fwd[0, t, z].astype(jnp.float32)
            hs = hs + temper * diff
            fx = fx + temper * (0.5 * (near[2] - near[3]))
            fy = fy + temper * (0.5 * (near[4] - near[5]))
        heat[z] = hs
        flow[0, z] = fx
        flow[1, z] = fy
        return 0

    def span(c):
        return pl.ds(c * per, per)

    def flow_copy(c):
        return pltpu.make_async_remote_copy(
            src_ref=flow.at[other, span(c)], dst_ref=flow_in.at[span(c)],
            send_sem=f_send.at[c], recv_sem=f_recv.at[c],
            device_id={"sec": other}, device_id_type=MESH,
        )

    def part_copy(c):
        return pltpu.make_async_remote_copy(
            src_ref=part.at[span(c)], dst_ref=part_in.at[span(c)],
            send_sem=p_send.at[c], recv_sem=p_recv.at[c],
            device_id={"sec": other}, device_id_type=MESH,
        )

    mine = pl.ds(gy * row_blocks, row_blocks)

    def gather_copy(c, off):
        return pltpu.make_async_remote_copy(
            src_ref=gath[c].at[mine], dst_ref=gath[c].at[mine],
            send_sem=g_send.at[c, off - 1], recv_sem=g_recv.at[c, off - 1],
            device_id={"gy": lax.rem(gy + off, n_gy)}, device_id_type=MESH,
        )

    def gather_recv(c, off):
        theirs = pl.ds(lax.rem(gy + n_gy - off, n_gy) * row_blocks, row_blocks)
        return pltpu.make_async_remote_copy(
            src_ref=gath[c].at[mine], dst_ref=gath[c].at[theirs],
            send_sem=g_send.at[c, off - 1], recv_sem=g_recv.at[c, off - 1],
            device_id={"gy": lax.rem(gy + off, n_gy)}, device_id_type=MESH,
        )

    def spread(c):
        flow_copy(c).wait()
        total = (flow[s, span(c)] + flow_in[span(c)]).astype(jnp.bfloat16)
        for b in range(row_blocks):
            gath[c][gy * row_blocks + b] = total[:, :, b * size:(b + 1) * size]
        for off in range(1, n_gy):
            gather_copy(c, off).start()

    for c in range(CHUNKS):
        lax.fori_loop(c * per, (c + 1) * per, second, 0)
        flow_copy(c).start()
        if c > 0:
            spread(c - 1)
    spread(CHUNKS - 1)

    def finish(c):
        part_copy(c).wait()
        sens[span(c)] = part[span(c)] + part_in[span(c)]

    for c in range(CHUNKS):
        for off in range(1, n_gy):
            gather_recv(c, off).wait()
        for r in range(row_blocks):
            left = jnp.concatenate(
                [gath[c][cols[r, k]].reshape(per * rows, size) for k in range(per_row)], axis=1
            )
            right = jnp.concatenate([blocks[r, k] for k in range(per_row)], axis=1)
            out = lax.dot_general(left, right, NT, preferred_element_type=jnp.float32)
            out = out.reshape(per, rows, size)
            lanes = slice(r * size, (r + 1) * size)
            head[0, span(c), :, lanes] = out
            part[span(c), :, lanes] = heat[span(c), :, lanes] + out * grad[
                0, span(c), :, lanes
            ].astype(jnp.float32)
        part_copy(c).start()
        if c > 0:
            finish(c - 1)
    finish(CHUNKS - 1)


def solution(mesh):
    n_sec, n_gx, n_gy = (mesh.shape[a] for a in ("sec", "gx", "gy"))
    assert n_sec == 2

    def shards(
        terminal, forward_temp, conductivity, velocity, fixed_mask, wells, misfit, head_gradient,
        blocks, block_cols,
    ):
        tests, layers, rows, width = terminal.shape
        row_blocks, _, size, _ = blocks.shape
        field = (layers, rows, width)
        vmem = pl.BlockSpec(memory_space=pltpu.VMEM)
        smem = pl.BlockSpec(memory_space=pltpu.SMEM)
        f32 = jnp.float32
        dma = pltpu.SemaphoreType.DMA
        return pl.pallas_call(
            functools.partial(kernel, n_gx, n_gy),
            out_shape=(
                jax.ShapeDtypeStruct((1,) + field, f32),
                jax.ShapeDtypeStruct(field, f32),
            ),
            in_specs=[smem] * 3 + [vmem] * 7,
            out_specs=(vmem, vmem),
            scratch_shapes=[
                pltpu.VMEM((6,) + field, f32),
                pltpu.VMEM((tests,) + field, f32),
                pltpu.VMEM(field, f32),
                pltpu.VMEM((2,) + field, f32),
                pltpu.VMEM(field, f32),
                pltpu.VMEM(field, f32),
                pltpu.VMEM(field, f32),
                pltpu.VMEM((2, tests + 1, layers, width), f32),
                pltpu.VMEM((2, rows, LANES), f32),
                pltpu.VMEM((2, tests + 1, layers, width), f32),
                pltpu.VMEM((2, rows, LANES), f32),
                pltpu.VMEM((2, tests, layers, width), f32),
                pltpu.VMEM((2, rows, LANES), f32),
                pltpu.VMEM((2, tests, layers, width), f32),
                pltpu.VMEM((2, rows, LANES), f32),
                dma((2, 4)), dma((2, 4)),
                dma((CHUNKS,)), dma((CHUNKS,)),
                dma((CHUNKS, n_gy - 1)), dma((CHUNKS, n_gy - 1)),
                dma((CHUNKS,)), dma((CHUNKS,)),
            ] + [
                pltpu.VMEM((n_gy * row_blocks, layers // CHUNKS, rows, size), jnp.bfloat16)
                for _ in range(CHUNKS)
            ],
            compiler_params=pltpu.CompilerParams(
                collective_id=0, has_side_effects=True, vmem_limit_bytes=40 * 1024 * 1024
            ),
        )(
            wells, misfit, block_cols, terminal, forward_temp, conductivity, velocity, fixed_mask,
            head_gradient, blocks,
        )

    placed = (
        P("sec", None, "gx", "gy"),
        P(None, "sec", None, "gx", "gy"),
        P(None, "gx", "gy"),
        P(None, None, "gx", "gy"),
        P(None, "gx", "gy"),
        P("sec", None, None),
        P(None, "sec", None),
        P("sec", None, "gx", "gy"),
        P("gy", None, None, None),
        P("gy", None),
    )
    return jax.shard_map(
        shards,
        mesh=mesh,
        in_specs=placed,
        out_specs=(P("sec", None, "gx", "gy"), P(None, "gx", "gy")),
        check_vma=False,
    )
```

```python
import functools

import jax
import jax.numpy as jnp
from jax import lax
from jax.experimental import pallas as pl
from jax.experimental.pallas import tpu as pltpu
from jax.sharding import PartitionSpec as P

MESH = pl.DeviceIdType.MESH
LANES = 128
CHUNKS = 4
NT = (((1,), (1,)), ((), ()))


def kernel(
    n_gx, n_gy, wells, misfit, cols,
    term_in, fwd_in, kappa_in, vel_in, mask_in, grad_in, blocks_in, head, sens,
    term, fwd, kappa, vel, mask, grad, blocks, in_sem, wgt, adj, heat, flow, flow_in, part, part_in,
    sx1, sy1, hx1, hy1, sx2, sy2, hx2, hy2,
    h_send, h_recv, f_send, f_recv, g_send, g_recv, p_send, p_recv, *gath,
):
    tests, layers, rows, width = term.shape
    row_blocks, per_row, size, _ = blocks.shape
    per = layers // CHUNKS
    s, gx, gy = lax.axis_index("sec"), lax.axis_index("gx"), lax.axis_index("gy")
    other = 1 - s
    exists = (gx > 0, gx < n_gx - 1, gy > 0, gy < n_gy - 1)
    target = (
        {"gx": jnp.maximum(gx - 1, 0)}, {"gx": jnp.minimum(gx + 1, n_gx - 1)},
        {"gy": jnp.maximum(gy - 1, 0)}, {"gy": jnp.minimum(gy + 1, n_gy - 1)},
    )

    row_id = lax.broadcasted_iota(jnp.int32, (rows, width), 0)
    col_id = lax.broadcasted_iota(jnp.int32, (rows, width), 1)
    lane = lax.broadcasted_iota(jnp.int32, (rows, LANES), 1)

    loads = {
        name: pltpu.make_async_copy(src, dst, in_sem.at[i])
        for i, (name, src, dst) in enumerate((
            ("term", term_in, term), ("kappa", kappa_in, kappa), ("vel", vel_in, vel),
            ("mask", mask_in, mask), ("fwd", fwd_in, fwd), ("grad", grad_in, grad),
            ("blocks", blocks_in, blocks),
        ))
    }
    for load in loads.values():
        load.start()

    barrier = pltpu.get_barrier_semaphore()
    for side in (0, 1):
        @pl.when(exists[side])
        def _(side=side):
            pl.semaphore_signal(barrier, 1, device_id=target[side], device_id_type=MESH)
    for off in range(1, n_gy):
        pl.semaphore_signal(barrier, 1, device_id={"gy": lax.rem(gy + off, n_gy)}, device_id_type=MESH)
    pl.semaphore_signal(barrier, 1, device_id={"sec": other}, device_id_type=MESH)

    def halo(round_, side, sx, sy, hx, hy):
        opposite = side ^ 1
        src = sx.at[side] if side < 2 else sy.at[side - 2]
        dst = hx.at[opposite] if side < 2 else hy.at[opposite - 2]
        return pltpu.make_async_remote_copy(
            src_ref=src, dst_ref=dst,
            send_sem=h_send.at[round_, side], recv_sem=h_recv.at[round_, opposite],
            device_id=target[side], device_id_type=MESH,
        )

    def halo_recv(round_, side, sx, sy, hx, hy):
        src = sx.at[side] if side < 2 else sy.at[side - 2]
        dst = hx.at[side] if side < 2 else hy.at[side - 2]
        return pltpu.make_async_remote_copy(
            src_ref=src, dst_ref=dst,
            send_sem=h_send.at[round_, side], recv_sem=h_recv.at[round_, side],
            device_id=target[side], device_id_type=MESH,
        )

    def start_halo(round_, bufs):
        for side in range(4):
            @pl.when(exists[side])
            def _(side=side):
                halo(round_, side, *bufs).start()

    def wait_halo(round_, bufs):
        for side in range(4):
            @pl.when(exists[side])
            def _(side=side):
                halo_recv(round_, side, *bufs).wait()

            @pl.when(jnp.logical_not(exists[side]))
            def _(side=side):
                into = bufs[2].at[side] if side < 2 else bufs[3].at[side - 2]
                into[...] = jnp.zeros(into.shape, jnp.float32)

    def planes_of(lo, hi, body, carry):
        def pair(i, carry):
            return body(lo + 2 * i + 1, body(lo + 2 * i, carry))

        return lax.fori_loop(0, (hi - lo) // 2, pair, carry)

    zero = jnp.zeros((rows, LANES), jnp.float32)

    def pack1(z, carry):
        low, high = carry
        planes = [term[t, z] for t in range(tests)] + [kappa[z]]
        for slot, plane in enumerate(planes):
            here = lane == slot * layers + z
            low = jnp.where(here, plane[:, 0:1], low)
            high = jnp.where(here, plane[:, width - 1:width], high)
            sx1[0, slot, pl.ds(z, 1), :] = plane[0:1, :]
            sx1[1, slot, pl.ds(z, 1), :] = plane[rows - 1:rows, :]
        return low, high

    loads["term"].wait()
    loads["kappa"].wait()
    low, high = planes_of(0, layers, pack1, (zero, zero))
    sy1[0] = low
    sy1[1] = high
    expected = n_gy + (gx > 0).astype(jnp.int32) + (gx < n_gx - 1).astype(jnp.int32)
    pl.semaphore_wait(barrier, expected)
    bufs1 = (sx1, sy1, hx1, hy1)
    half = layers // 2
    bufs2 = [tuple(ref.at[h] for ref in (sx2, sy2, hx2, hy2)) for h in range(2)]
    start_halo(0, bufs1)

    cell = row_id * width + col_id
    plane_cells = rows * width
    marks = []
    for t in range(tests):
        for w in range(wells.shape[2]):
            lx = wells[1, t, w] - gx * rows
            ly = wells[2, t, w] - gy * width
            inside = (lx >= 0) & (lx < rows) & (ly >= 0) & (ly < width)
            place = wells[0, t, w] * plane_cells + lx * width + ly
            marks.append(jnp.where(inside, place, -1))

    def sources(z, _):
        now = cell + z * plane_cells
        for t in range(tests):
            total = jnp.zeros((rows, width), jnp.float32)
            for w in range(wells.shape[2]):
                total = total + jnp.where(now == marks[t * wells.shape[2] + w], misfit[1, t, w], 0.0)
            adj[t, z] = total
        return 0

    planes_of(0, layers, sources, 0)
    for name in ("vel", "mask", "fwd"):
        loads[name].wait()
    wait_halo(0, bufs1)

    def moved_lane(ref, side, shift):
        return jnp.concatenate([pltpu.roll(ref[side], shift, 1)] * (width // LANES), axis=1)

    def beside(plane, hx, hy, slot, z, depth):
        xp = jnp.where(row_id == rows - 1, hx[1, slot, pl.ds(z, 1), :], pltpu.roll(plane, rows - 1, 0))
        xm = jnp.where(row_id == 0, hx[0, slot, pl.ds(z, 1), :], pltpu.roll(plane, 1, 0))
        index = slot * depth + z
        up, down = LANES - 1 - index, lax.rem(LANES - index, LANES)
        yp = jnp.where(col_id == width - 1, moved_lane(hy, 1, up), pltpu.roll(plane, width - 1, 1))
        ym = jnp.where(col_id == 0, moved_lane(hy, 0, down), pltpu.roll(plane, 1, 1))
        return xp, xm, yp, ym

    def harmonic(a, b):
        return 2.0 * a * b / (a + b)

    def first(h, z, carry):
        low, high = carry
        zp, zm = jnp.minimum(z + 1, layers - 1), jnp.maximum(z - 1, 0)
        k = kappa[z]
        weights = [harmonic(k, kappa[zp]), harmonic(k, kappa[zm])]
        weights += [harmonic(k, near) for near in beside(k, hx1, hy1, tests, z, layers)]
        for face in range(6):
            wgt[face, z] = weights[face]
        keep = 1.0 - mask[z].astype(jnp.float32)
        hs = jnp.zeros((rows, width), jnp.float32)
        fx, fy = hs, hs
        for t in range(tests):
            c = term[t, z]
            near = (term[t, zp], term[t, zm]) + beside(c, hx1, hy1, t, z, layers)
            diff = weights[0] * (near[0] - c)
            for face in range(1, 6):
                diff = diff + weights[face] * (near[face] - c)
            slope_x = 0.5 * (near[2] - near[3])
            slope_y = 0.5 * (near[4] - near[5])
            new = keep * (c + diff + vel[0, z] * slope_x + vel[1, z] * slope_y + adj[t, z])
            adj[t, z] = new
            here = lane == t * half + (z - h * half)
            low = jnp.where(here, new[:, 0:1], low)
            high = jnp.where(here, new[:, width - 1:width], high)
            sx2[h, 0, t, pl.ds(z - h * half, 1), :] = new[0:1, :]
            sx2[h, 1, t, pl.ds(z - h * half, 1), :] = new[rows - 1:rows, :]
            temper = fwd[1, t, z].astype(jnp.float32)
            hs = hs + temper * diff
            fx = fx + temper * slope_x
            fy = fy + temper * slope_y
        heat[z] = hs
        flow[0, z] = fx
        flow[1, z] = fy
        return low, high

    for h in range(2):
        low, high = planes_of(h * half, (h + 1) * half, functools.partial(first, h), (zero, zero))
        sy2[h, 0] = low
        sy2[h, 1] = high
        start_halo(1 + h, bufs2[h])

    def second(h, z, _):
        zp, zm = jnp.minimum(z + 1, layers - 1), jnp.maximum(z - 1, 0)
        hs, fx, fy = heat[z], flow[0, z], flow[1, z]
        for t in range(tests):
            c = adj[t, z]
            near = (adj[t, zp], adj[t, zm]) + beside(c, hx2.at[h], hy2.at[h], t, z - h * half, half)
            diff = wgt[0, z] * (near[0] - c)
            for face in range(1, 6):
                diff = diff + wgt[face, z] * (near[face] - c)
            temper = fwd[0, t, z].astype(jnp.float32)
            hs = hs + temper * diff
            fx = fx + temper * (0.5 * (near[2] - near[3]))
            fy = fy + temper * (0.5 * (near[4] - near[5]))
        heat[z] = hs
        flow[0, z] = fx
        flow[1, z] = fy
        return 0

    def span(c):
        return pl.ds(c * per, per)

    def flow_copy(c):
        return pltpu.make_async_remote_copy(
            src_ref=flow.at[other, span(c)], dst_ref=flow_in.at[span(c)],
            send_sem=f_send.at[c], recv_sem=f_recv.at[c],
            device_id={"sec": other}, device_id_type=MESH,
        )

    def part_copy(c):
        return pltpu.make_async_remote_copy(
            src_ref=part.at[span(c)], dst_ref=part_in.at[span(c)],
            send_sem=p_send.at[c], recv_sem=p_recv.at[c],
            device_id={"sec": other}, device_id_type=MESH,
        )

    mine = pl.ds(gy * row_blocks, row_blocks)

    def gather_copy(c, off):
        return pltpu.make_async_remote_copy(
            src_ref=gath[c].at[mine], dst_ref=gath[c].at[mine],
            send_sem=g_send.at[c, off - 1], recv_sem=g_recv.at[c, off - 1],
            device_id={"gy": lax.rem(gy + off, n_gy)}, device_id_type=MESH,
        )

    def gather_recv(c, off):
        theirs = pl.ds(lax.rem(gy + n_gy - off, n_gy) * row_blocks, row_blocks)
        return pltpu.make_async_remote_copy(
            src_ref=gath[c].at[mine], dst_ref=gath[c].at[theirs],
            send_sem=g_send.at[c, off - 1], recv_sem=g_recv.at[c, off - 1],
            device_id={"gy": lax.rem(gy + off, n_gy)}, device_id_type=MESH,
        )

    def spread(c):
        flow_copy(c).wait()
        total = (flow[s, span(c)] + flow_in[span(c)]).astype(jnp.bfloat16)
        for b in range(row_blocks):
            gath[c][gy * row_blocks + b] = total[:, :, b * size:(b + 1) * size]
        for off in range(1, n_gy):
            gather_copy(c, off).start()

    for c in range(CHUNKS):
        h = c // (CHUNKS // 2)
        if c % (CHUNKS // 2) == 0:
            wait_halo(1 + h, bufs2[h])
        planes_of(c * per, (c + 1) * per, functools.partial(second, h), 0)
        flow_copy(c).start()
        if c > 0:
            spread(c - 1)
    spread(CHUNKS - 1)

    loads["grad"].wait()
    loads["blocks"].wait()

    def finish(c):
        part_copy(c).wait()
        sens[span(c)] = part[span(c)] + part_in[span(c)]

    for c in range(CHUNKS):
        for off in range(1, n_gy):
            gather_recv(c, off).wait()
        for r in range(row_blocks):
            left = jnp.concatenate(
                [gath[c][cols[r, k]].reshape(per * rows, size) for k in range(per_row)], axis=1
            )
            right = jnp.concatenate([blocks[r, k] for k in range(per_row)], axis=1)
            out = lax.dot_general(left, right, NT, preferred_element_type=jnp.float32)
            out = out.reshape(per, rows, size)
            lanes = slice(r * size, (r + 1) * size)
            head[0, span(c), :, lanes] = out
            part[span(c), :, lanes] = heat[span(c), :, lanes] + out * grad[
                0, span(c), :, lanes
            ].astype(jnp.float32)
        part_copy(c).start()
        if c > 0:
            finish(c - 1)
    finish(CHUNKS - 1)


def solution(mesh):
    n_sec, n_gx, n_gy = (mesh.shape[a] for a in ("sec", "gx", "gy"))
    assert n_sec == 2

    def shards(
        terminal, forward_temp, conductivity, velocity, fixed_mask, wells, misfit, head_gradient,
        blocks, block_cols,
    ):
        tests, layers, rows, width = terminal.shape
        row_blocks, _, size, _ = blocks.shape
        field = (layers, rows, width)
        vmem = pl.BlockSpec(memory_space=pltpu.VMEM)
        hbm = pl.BlockSpec(memory_space=pltpu.HBM)
        smem = pl.BlockSpec(memory_space=pltpu.SMEM)
        f32 = jnp.float32
        dma = pltpu.SemaphoreType.DMA
        return pl.pallas_call(
            functools.partial(kernel, n_gx, n_gy),
            out_shape=(
                jax.ShapeDtypeStruct((1,) + field, f32),
                jax.ShapeDtypeStruct(field, f32),
            ),
            in_specs=[smem] * 3 + [hbm] * 7,
            out_specs=(vmem, vmem),
            scratch_shapes=[
                pltpu.VMEM(a.shape, a.dtype)
                for a in (
                    terminal, forward_temp, conductivity, velocity, fixed_mask, head_gradient, blocks
                )
            ] + [
                dma((7,)),
                pltpu.VMEM((6,) + field, f32),
                pltpu.VMEM((tests,) + field, f32),
                pltpu.VMEM(field, f32),
                pltpu.VMEM((2,) + field, f32),
                pltpu.VMEM(field, f32),
                pltpu.VMEM(field, f32),
                pltpu.VMEM(field, f32),
                pltpu.VMEM((2, tests + 1, layers, width), f32),
                pltpu.VMEM((2, rows, LANES), f32),
                pltpu.VMEM((2, tests + 1, layers, width), f32),
                pltpu.VMEM((2, rows, LANES), f32),
                pltpu.VMEM((2, 2, tests, layers // 2, width), f32),
                pltpu.VMEM((2, 2, rows, LANES), f32),
                pltpu.VMEM((2, 2, tests, layers // 2, width), f32),
                pltpu.VMEM((2, 2, rows, LANES), f32),
                dma((3, 4)), dma((3, 4)),
                dma((CHUNKS,)), dma((CHUNKS,)),
                dma((CHUNKS, n_gy - 1)), dma((CHUNKS, n_gy - 1)),
                dma((CHUNKS,)), dma((CHUNKS,)),
            ] + [
                pltpu.VMEM((n_gy * row_blocks, layers // CHUNKS, rows, size), jnp.bfloat16)
                for _ in range(CHUNKS)
            ],
            compiler_params=pltpu.CompilerParams(
                collective_id=0, has_side_effects=True, vmem_limit_bytes=40 * 1024 * 1024
            ),
        )(
            jnp.transpose(wells, (2, 0, 1)), misfit, block_cols, terminal, forward_temp, conductivity, velocity, fixed_mask,
            head_gradient, blocks,
        )

    placed = (
        P("sec", None, "gx", "gy"),
        P(None, "sec", None, "gx", "gy"),
        P(None, "gx", "gy"),
        P(None, None, "gx", "gy"),
        P(None, "gx", "gy"),
        P("sec", None, None),
        P(None, "sec", None),
        P("sec", None, "gx", "gy"),
        P("gy", None, None, None),
        P("gy", None),
    )
    return jax.shard_map(
        shards,
        mesh=mesh,
        in_specs=placed,
        out_specs=(P("sec", None, "gx", "gy"), P(None, "gx", "gy")),
        check_vma=False,
    )
```

```python
import functools

import jax
import jax.numpy as jnp
from jax import lax
from jax.experimental import pallas as pl
from jax.experimental.pallas import tpu as pltpu
from jax.sharding import PartitionSpec as P

MESH = pl.DeviceIdType.MESH
LANES = 128
CHUNKS = 4
NT = (((1,), (1,)), ((), ()))


def kernel(
    n_gx, n_gy, wells, misfit, cols,
    term_in, fwd_in, kappa_in, vel_in, mask_in, grad_in, blocks_in, head, sens,
    term, fwd, kappa, vel, mask, grad, blocks, in_sem, wgt, adj, heat, flow, flow_in, part, part_in,
    sx1, sy1, hx1, hy1, sx2, sy2, hx2, hy2,
    h_send, h_recv, f_send, f_recv, g_send, g_recv, p_send, p_recv, *gath,
):
    tests, layers, rows, width = term.shape
    row_blocks, per_row, size, _ = blocks.shape
    per = layers // CHUNKS
    s, gx, gy = lax.axis_index("sec"), lax.axis_index("gx"), lax.axis_index("gy")
    other = 1 - s
    exists = (gx > 0, gx < n_gx - 1, gy > 0, gy < n_gy - 1)
    target = (
        {"gx": jnp.maximum(gx - 1, 0)}, {"gx": jnp.minimum(gx + 1, n_gx - 1)},
        {"gy": jnp.maximum(gy - 1, 0)}, {"gy": jnp.minimum(gy + 1, n_gy - 1)},
    )

    row_id = lax.broadcasted_iota(jnp.int32, (rows, width), 0)
    col_id = lax.broadcasted_iota(jnp.int32, (rows, width), 1)
    lane = lax.broadcasted_iota(jnp.int32, (rows, LANES), 1)

    loads = {
        name: pltpu.make_async_copy(src, dst, in_sem.at[i])
        for i, (name, src, dst) in enumerate((
            ("term", term_in, term), ("kappa", kappa_in, kappa), ("vel", vel_in, vel),
            ("mask", mask_in, mask), ("fwd", fwd_in, fwd), ("grad", grad_in, grad),
            ("blocks", blocks_in, blocks),
        ))
    }
    for load in loads.values():
        load.start()

    barrier = pltpu.get_barrier_semaphore()
    for side in (0, 1):
        @pl.when(exists[side])
        def _(side=side):
            pl.semaphore_signal(barrier, 1, device_id=target[side], device_id_type=MESH)
    for off in range(1, n_gy):
        pl.semaphore_signal(barrier, 1, device_id={"gy": lax.rem(gy + off, n_gy)}, device_id_type=MESH)
    pl.semaphore_signal(barrier, 1, device_id={"sec": other}, device_id_type=MESH)

    def halo(round_, side, sx, sy, hx, hy):
        opposite = side ^ 1
        src = sx.at[side] if side < 2 else sy.at[side - 2]
        dst = hx.at[opposite] if side < 2 else hy.at[opposite - 2]
        return pltpu.make_async_remote_copy(
            src_ref=src, dst_ref=dst,
            send_sem=h_send.at[round_, side], recv_sem=h_recv.at[round_, opposite],
            device_id=target[side], device_id_type=MESH,
        )

    def halo_recv(round_, side, sx, sy, hx, hy):
        src = sx.at[side] if side < 2 else sy.at[side - 2]
        dst = hx.at[side] if side < 2 else hy.at[side - 2]
        return pltpu.make_async_remote_copy(
            src_ref=src, dst_ref=dst,
            send_sem=h_send.at[round_, side], recv_sem=h_recv.at[round_, side],
            device_id=target[side], device_id_type=MESH,
        )

    def start_halo(round_, bufs):
        for side in range(4):
            @pl.when(exists[side])
            def _(side=side):
                halo(round_, side, *bufs).start()

    def wait_halo(round_, bufs):
        for side in range(4):
            @pl.when(exists[side])
            def _(side=side):
                halo_recv(round_, side, *bufs).wait()

            @pl.when(jnp.logical_not(exists[side]))
            def _(side=side):
                into = bufs[2].at[side] if side < 2 else bufs[3].at[side - 2]
                into[...] = jnp.zeros(into.shape, jnp.float32)

    def planes_of(lo, hi, body, carry):
        def pair(i, carry):
            return body(lo + 2 * i + 1, body(lo + 2 * i, carry))

        return lax.fori_loop(0, (hi - lo) // 2, pair, carry)

    zero = jnp.zeros((rows, LANES), jnp.float32)

    def pack1(z, carry):
        low, high = carry
        planes = [term[t, z] for t in range(tests)] + [kappa[z]]
        for slot, plane in enumerate(planes):
            here = lane == slot * layers + z
            low = jnp.where(here, plane[:, 0:1], low)
            high = jnp.where(here, plane[:, width - 1:width], high)
            sx1[0, slot, pl.ds(z, 1), :] = plane[0:1, :]
            sx1[1, slot, pl.ds(z, 1), :] = plane[rows - 1:rows, :]
        return low, high

    loads["term"].wait()
    loads["kappa"].wait()
    low, high = planes_of(0, layers, pack1, (zero, zero))
    sy1[0] = low
    sy1[1] = high
    expected = n_gy + (gx > 0).astype(jnp.int32) + (gx < n_gx - 1).astype(jnp.int32)
    pl.semaphore_wait(barrier, expected)
    bufs1 = (sx1, sy1, hx1, hy1)
    half = layers // 2
    bufs2 = [tuple(ref.at[h] for ref in (sx2, sy2, hx2, hy2)) for h in range(2)]
    start_halo(0, bufs1)

    cell = row_id * width + col_id
    plane_cells = rows * width
    marks = []
    for t in range(tests):
        for w in range(wells.shape[2]):
            lx = wells[1, t, w] - gx * rows
            ly = wells[2, t, w] - gy * width
            inside = (lx >= 0) & (lx < rows) & (ly >= 0) & (ly < width)
            place = wells[0, t, w] * plane_cells + lx * width + ly
            marks.append(jnp.where(inside, place, -1))

    def sources(z, _):
        now = cell + z * plane_cells
        for t in range(tests):
            total = jnp.zeros((rows, width), jnp.float32)
            for w in range(wells.shape[2]):
                total = total + jnp.where(now == marks[t * wells.shape[2] + w], misfit[1, t, w], 0.0)
            adj[t, z] = total
        return 0

    planes_of(0, layers, sources, 0)
    for name in ("vel", "mask", "fwd"):
        loads[name].wait()
    wait_halo(0, bufs1)

    def moved_lane(ref, side, shift):
        return jnp.concatenate([pltpu.roll(ref[side], shift, 1)] * (width // LANES), axis=1)

    def beside(plane, hx, hy, slot, z, depth):
        xp = jnp.where(row_id == rows - 1, hx[1, slot, pl.ds(z, 1), :], pltpu.roll(plane, rows - 1, 0))
        xm = jnp.where(row_id == 0, hx[0, slot, pl.ds(z, 1), :], pltpu.roll(plane, 1, 0))
        index = slot * depth + z
        up, down = LANES - 1 - index, lax.rem(LANES - index, LANES)
        yp = jnp.where(col_id == width - 1, moved_lane(hy, 1, up), pltpu.roll(plane, width - 1, 1))
        ym = jnp.where(col_id == 0, moved_lane(hy, 0, down), pltpu.roll(plane, 1, 1))
        return xp, xm, yp, ym

    def harmonic(a, b):
        return 2.0 * a * b / (a + b)

    def first(h, z, carry):
        low, high = carry
        zp, zm = jnp.minimum(z + 1, layers - 1), jnp.maximum(z - 1, 0)
        k = kappa[z]
        weights = [harmonic(k, kappa[zp]), harmonic(k, kappa[zm])]
        weights += [harmonic(k, near) for near in beside(k, hx1, hy1, tests, z, layers)]
        for face in range(6):
            wgt[face, z] = weights[face]
        keep = 1.0 - mask[z].astype(jnp.float32)
        hs = jnp.zeros((rows, width), jnp.float32)
        fx, fy = hs, hs
        for t in range(tests):
            c = term[t, z]
            near = (term[t, zp], term[t, zm]) + beside(c, hx1, hy1, t, z, layers)
            diff = weights[0] * (near[0] - c)
            for face in range(1, 6):
                diff = diff + weights[face] * (near[face] - c)
            slope_x = 0.5 * (near[2] - near[3])
            slope_y = 0.5 * (near[4] - near[5])
            new = keep * (c + diff + vel[0, z] * slope_x + vel[1, z] * slope_y + adj[t, z])
            adj[t, z] = new
            here = lane == t * half + (z - h * half)
            low = jnp.where(here, new[:, 0:1], low)
            high = jnp.where(here, new[:, width - 1:width], high)
            sx2[h, 0, t, pl.ds(z - h * half, 1), :] = new[0:1, :]
            sx2[h, 1, t, pl.ds(z - h * half, 1), :] = new[rows - 1:rows, :]
            temper = fwd[1, t, z].astype(jnp.float32)
            hs = hs + temper * diff
            fx = fx + temper * slope_x
            fy = fy + temper * slope_y
        heat[z] = hs
        flow[0, z] = fx
        flow[1, z] = fy
        return low, high

    for h in range(2):
        low, high = planes_of(h * half, (h + 1) * half, functools.partial(first, h), (zero, zero))
        sy2[h, 0] = low
        sy2[h, 1] = high
        start_halo(1 + h, bufs2[h])

    def second(h, z, _):
        zp, zm = jnp.minimum(z + 1, layers - 1), jnp.maximum(z - 1, 0)
        hs, fx, fy = heat[z], flow[0, z], flow[1, z]
        for t in range(tests):
            c = adj[t, z]
            near = (adj[t, zp], adj[t, zm]) + beside(c, hx2.at[h], hy2.at[h], t, z - h * half, half)
            diff = wgt[0, z] * (near[0] - c)
            for face in range(1, 6):
                diff = diff + wgt[face, z] * (near[face] - c)
            temper = fwd[0, t, z].astype(jnp.float32)
            hs = hs + temper * diff
            fx = fx + temper * (0.5 * (near[2] - near[3]))
            fy = fy + temper * (0.5 * (near[4] - near[5]))
        heat[z] = hs
        flow[0, z] = fx
        flow[1, z] = fy
        return 0

    def span(c):
        return pl.ds(c * per, per)

    def flow_copy(c):
        return pltpu.make_async_remote_copy(
            src_ref=flow.at[other, span(c)], dst_ref=flow_in.at[span(c)],
            send_sem=f_send.at[c], recv_sem=f_recv.at[c],
            device_id={"sec": other}, device_id_type=MESH,
        )

    def part_copy(c):
        return pltpu.make_async_remote_copy(
            src_ref=part.at[span(c)], dst_ref=part_in.at[span(c)],
            send_sem=p_send.at[c], recv_sem=p_recv.at[c],
            device_id={"sec": other}, device_id_type=MESH,
        )

    mine = pl.ds(gy * row_blocks, row_blocks)

    def gather_copy(c, off):
        return pltpu.make_async_remote_copy(
            src_ref=gath[c].at[mine], dst_ref=gath[c].at[mine],
            send_sem=g_send.at[c, off - 1], recv_sem=g_recv.at[c, off - 1],
            device_id={"gy": lax.rem(gy + off, n_gy)}, device_id_type=MESH,
        )

    def gather_recv(c, off):
        theirs = pl.ds(lax.rem(gy + n_gy - off, n_gy) * row_blocks, row_blocks)
        return pltpu.make_async_remote_copy(
            src_ref=gath[c].at[mine], dst_ref=gath[c].at[theirs],
            send_sem=g_send.at[c, off - 1], recv_sem=g_recv.at[c, off - 1],
            device_id={"gy": lax.rem(gy + off, n_gy)}, device_id_type=MESH,
        )

    def spread(c):
        flow_copy(c).wait()
        total = (flow[s, span(c)] + flow_in[span(c)]).astype(jnp.bfloat16)
        for b in range(row_blocks):
            gath[c][gy * row_blocks + b] = total[:, :, b * size:(b + 1) * size]
        for off in range(1, n_gy):
            gather_copy(c, off).start()

    for c in range(CHUNKS):
        h = c // (CHUNKS // 2)
        if c % (CHUNKS // 2) == 0:
            wait_halo(1 + h, bufs2[h])
        planes_of(c * per, (c + 1) * per, functools.partial(second, h), 0)
        flow_copy(c).start()
        if c > 0:
            spread(c - 1)
    spread(CHUNKS - 1)

    loads["grad"].wait()
    loads["blocks"].wait()

    def finish(c):
        part_copy(c).wait()
        sens[span(c)] = part[span(c)] + part_in[span(c)]

    for c in range(CHUNKS):
        for off in range(1, n_gy):
            gather_recv(c, off).wait()
        for r in range(row_blocks):
            left = jnp.concatenate(
                [gath[c][cols[r, k]].reshape(per * rows, size) for k in range(per_row)], axis=1
            )
            right = jnp.concatenate([blocks[r, k] for k in range(per_row)], axis=1)
            out = lax.dot_general(left, right, NT, preferred_element_type=jnp.float32)
            out = out.reshape(per, rows, size)
            lanes = slice(r * size, (r + 1) * size)
            head[0, span(c), :, lanes] = out
            part[span(c), :, lanes] = heat[span(c), :, lanes] + out * grad[
                0, span(c), :, lanes
            ].astype(jnp.float32)
        part_copy(c).start()
        if c > 0:
            finish(c - 1)
    finish(CHUNKS - 1)


def solution(mesh):
    n_sec, n_gx, n_gy = (mesh.shape[a] for a in ("sec", "gx", "gy"))
    assert n_sec == 2

    def shards(
        terminal, forward_temp, conductivity, velocity, fixed_mask, wells, misfit, head_gradient,
        blocks, block_cols,
    ):
        tests, layers, rows, width = terminal.shape
        row_blocks, _, size, _ = blocks.shape
        field = (layers, rows, width)
        vmem = pl.BlockSpec(memory_space=pltpu.VMEM)
        hbm = pl.BlockSpec(memory_space=pltpu.HBM)
        smem = pl.BlockSpec(memory_space=pltpu.SMEM)
        f32 = jnp.float32
        dma = pltpu.SemaphoreType.DMA
        return pl.pallas_call(
            functools.partial(kernel, n_gx, n_gy),
            out_shape=(
                jax.ShapeDtypeStruct((1,) + field, f32),
                jax.ShapeDtypeStruct(field, f32),
            ),
            in_specs=[smem] * 3 + [hbm] * 7,
            out_specs=(vmem, vmem),
            scratch_shapes=[
                pltpu.VMEM(a.shape, a.dtype)
                for a in (
                    terminal, forward_temp, conductivity, velocity, fixed_mask, head_gradient, blocks
                )
            ] + [
                dma((7,)),
                pltpu.VMEM((6,) + field, f32),
                pltpu.VMEM((tests,) + field, f32),
                pltpu.VMEM(field, f32),
                pltpu.VMEM((2,) + field, f32),
                pltpu.VMEM(field, f32),
                pltpu.VMEM(field, f32),
                pltpu.VMEM(field, f32),
                pltpu.VMEM((2, tests + 1, layers, width), f32),
                pltpu.VMEM((2, rows, LANES), f32),
                pltpu.VMEM((2, tests + 1, layers, width), f32),
                pltpu.VMEM((2, rows, LANES), f32),
                pltpu.VMEM((2, 2, tests, layers // 2, width), f32),
                pltpu.VMEM((2, 2, rows, LANES), f32),
                pltpu.VMEM((2, 2, tests, layers // 2, width), f32),
                pltpu.VMEM((2, 2, rows, LANES), f32),
                dma((3, 4)), dma((3, 4)),
                dma((CHUNKS,)), dma((CHUNKS,)),
                dma((CHUNKS, n_gy - 1)), dma((CHUNKS, n_gy - 1)),
                dma((CHUNKS,)), dma((CHUNKS,)),
            ] + [
                pltpu.VMEM((n_gy * row_blocks, layers // CHUNKS, rows, size), jnp.bfloat16)
                for _ in range(CHUNKS)
            ],
            compiler_params=pltpu.CompilerParams(
                collective_id=0, has_side_effects=True, vmem_limit_bytes=62 * 1024 * 1024
            ),
        )(
            jnp.transpose(wells, (2, 0, 1)), misfit, block_cols, terminal, forward_temp, conductivity, velocity, fixed_mask,
            head_gradient, blocks,
        )

    placed = (
        P("sec", None, "gx", "gy"),
        P(None, "sec", None, "gx", "gy"),
        P(None, "gx", "gy"),
        P(None, None, "gx", "gy"),
        P(None, "gx", "gy"),
        P("sec", None, None),
        P(None, "sec", None),
        P("sec", None, "gx", "gy"),
        P("gy", None, None, None),
        P("gy", None),
    )
    return jax.shard_map(
        shards,
        mesh=mesh,
        in_specs=placed,
        out_specs=(P("sec", None, "gx", "gy"), P(None, "gx", "gy")),
        check_vma=False,
    )
```
